128 devices in a mesh: node: 16 (over z_hi, x, core), local: 8 (over z_lo, y).
Axes of the slice: x: 4, y: 4, z: 4 (z_hi: 2, z_lo: 2; z = z_hi * 2 + z_lo), core: 2. Of those that a mesh axis runs over, the one named last changes fastest.
Arguments:
- image_embed: float32 [40960, 1152], P(('node', 'local')), may hold values from -1 to 1
- text_embed: float32 [40960, 1152], P(('node', 'local')), may hold values from -1 to 1
- logit_scale: float32 [], replicated, may hold values from 8 to 16
- logit_bias: float32 [], replicated, may hold values from -7 to -4
Outputs:
- image_grad: float32 [40960, 1152], P(('node', 'local'))
- text_grad: float32 [40960, 1152], P(('node', 'local'))
The draws below stay inside these ranges and needn't reach their ends.
All inputs are finite; a program needn't handle non-finite values.
Results may differ from the reference program's by a relative error of at most 0.0014.
Values may be sent and summed in bfloat16 or wider, within the bound.
A program may use at most 128 MiB of HBM per device.

```python
import math
import jax
import jax.numpy as jnp
from jax import lax

D = 1152
PAIRS = 40960
N_NODE = 16


def shared_part(key, weight_cluster, weight_pair):
    cluster_total = 32
    centers = jnp.clip(jax.random.normal(jax.random.fold_in(key, 11), (cluster_total, D), jnp.float32), -4.0, 4.0) * D ** (-0.5)
    labels = jax.random.randint(jax.random.fold_in(key, 12), (PAIRS,), 0, cluster_total)
    chosen = jnp.take(centers, labels, axis=0)
    pair_part = jnp.clip(jax.random.normal(jax.random.fold_in(key, 13), (PAIRS, D), jnp.float32), -4.0, 4.0) * D ** (-0.5)
    return weight_cluster * chosen + weight_pair * pair_part


def draw_image_embed(key, part):
    base = shared_part(key, 0.45, 0.55)
    key = jax.random.fold_in(key, 3)
    noise = jnp.clip(jax.random.normal(key, (PAIRS, D), jnp.float32), -4.0, 4.0) * D ** (-0.5)
    return base + 0.7 * noise


def draw_text_embed(key, part):
    base = shared_part(key, 0.45, 0.55)
    key = jax.random.fold_in(key, 5)
    noise = jnp.clip(jax.random.normal(key, (PAIRS, D), jnp.float32), -4.0, 4.0) * D ** (-0.5)
    return base + 0.7 * noise


def setup_inputs(seed: int = 0) -> dict:
    key_list = jax.random.split(jax.random.key(seed), 5)
    image_embed = draw_image_embed(jax.random.fold_in(key_list[4], 71), 0)
    text_embed = draw_text_embed(jax.random.fold_in(key_list[4], 71), 0)
    logit_scale = jnp.clip(jnp.exp(jax.random.uniform(key_list[2], (), jnp.float32, math.log(8.0), math.log(16.0))), 8.0, 16.0)
    logit_bias = jnp.clip(jax.random.uniform(key_list[3], (), jnp.float32, -7.0, -4.0), -7.0, -4.0)
    return dict(image_embed=image_embed, text_embed=text_embed, logit_scale=logit_scale, logit_bias=logit_bias)


def reference(image_embed, text_embed, logit_scale, logit_bias):
    image_half = image_embed.astype(jnp.bfloat16)
    text_half = text_embed.astype(jnp.bfloat16)
    width = image_half.shape[1]
    nodes = N_NODE
    group = image_half.shape[0] // nodes
    images = image_half.reshape(nodes, group, width)
    texts = text_half.reshape(nodes, group, width)
    earlier = jnp.roll(texts, 1, axis=0)
    match = jnp.concatenate([jnp.zeros((group, group), jnp.float32), jnp.eye(group, dtype=jnp.float32)], axis=1)

    def one_group(items):
        image_rows, own_rows, before_rows = items
        block = jnp.concatenate([before_rows, own_rows], axis=0)
        logits = logit_scale * lax.dot_general(image_rows, block, (((1,), (1,)), ((), ())), preferred_element_type=jnp.float32) + logit_bias
        coef = (logit_scale * (jax.nn.sigmoid(logits) - match)).astype(jnp.bfloat16)
        image_part = jnp.dot(coef, block, preferred_element_type=jnp.float32)
        text_part = lax.dot_general(coef, image_rows, (((0,), (0,)), ((), ())), preferred_element_type=jnp.float32)
        return image_part, text_part[group:], text_part[:group]

    image_parts, own_parts, before_parts = lax.map(one_group, (images, texts, earlier))
    image_grad = image_parts.reshape(nodes * group, width)
    text_grad = (own_parts + jnp.roll(before_parts, -1, axis=0)).reshape(nodes * group, width)
    return image_grad, text_grad
```

```python
import jax
import jax.numpy as jnp
from jax import lax
from jax.experimental import pallas as pl
from jax.experimental.pallas import tpu as pltpu
from jax.sharding import PartitionSpec as P

MESH = pl.DeviceIdType.MESH
ROWS, WIDTH = 320, 1152
HALF, PIECE = ROWS // 2, ROWS // 4
BLOCK = 4 * ROWS
NT = (((1,), (1,)), ((), ()))
TN = (((0,), (0,)), ((), ()))


def neighbours():
    node, local = lax.axis_index("node"), lax.axis_index("local")
    z_hi, x, core = node // 8, (node // 2) % 4, node % 2
    z_lo, y = local // 4, local % 4
    right = (node, z_lo * 4 + (y + 1) % 4)
    left = (node, z_lo * 4 + (y + 3) % 4)
    partner = (node, (1 - z_lo) * 4 + y)
    first = jnp.logical_and(core == 0, x == 0)
    last = jnp.logical_and(core == 1, x == 3)
    flipped = (1 - z_lo) * 4 + y
    before = ((node + 15) % 16, jnp.where(first, flipped, local))
    after = ((node + 1) % 16, jnp.where(last, flipped, local))
    return right, left, partner, before, after


def packed(value):
    square = value * value
    return (square * (value * jnp.abs(value))).astype(jnp.bfloat16)


def unpacked(power):
    power = power.astype(jnp.float32)
    root = lax.rsqrt(jnp.maximum(jnp.abs(power), 1e-37))
    return (power * root) * (root * lax.rsqrt(root))


def kernel(
    scale_ref, bias_ref, image_hbm, text_hbm, image_out, text_out,
    image_in, text_in, texts, images, coef, text_part, image_part,
    text_send, image_send, mid_recv, right_recv, left_recv, zn_recv, dn_recv, z_recv,
    image_sum, text_sum, load_sem, store_sem, send_sem, recv_sem,
):
    right, left, partner, before, after = neighbours()
    scale, bias = scale_ref[0], bias_ref[0]
    load_text = pltpu.make_async_copy(text_hbm, text_in, load_sem.at[0])
    load_image = pltpu.make_async_copy(image_hbm, image_in, load_sem.at[1])
    load_text.start()
    load_image.start()
    barrier = pltpu.get_barrier_semaphore()
    for device in (right, left, partner, before, after):
        pl.semaphore_signal(barrier, 1, device_id=device, device_id_type=MESH)

    copies = []

    def send(device, source, source_row, target, target_row, rows):
        k = len(copies)
        copy = pltpu.make_async_remote_copy(
            src_ref=source.at[pl.ds(source_row, rows)],
            dst_ref=target.at[pl.ds(target_row, rows)],
            send_sem=send_sem.at[k],
            recv_sem=recv_sem.at[k],
            device_id=device,
            device_id_type=MESH,
        )
        copy.start()
        copies.append(copy)
        return copy

    def coefficients(group, pair):
        block = texts[pl.ds(group * ROWS, ROWS), :]
        logits = scale * lax.dot_general(
            block, images[pl.ds(pair * 2 * ROWS, 2 * ROWS), :], NT, preferred_element_type=jnp.float32
        ) + bias
        value = 1.0 / (1.0 + jnp.exp(-logits))
        if group == 0 and pair == 0:
            shape = (ROWS, 2 * ROWS)
            match = lax.broadcasted_iota(jnp.int32, shape, 0) == lax.broadcasted_iota(jnp.int32, shape, 1)
            value = value - match.astype(jnp.float32)
        coef[pl.ds(group * ROWS, ROWS), pl.ds(pair * 2 * ROWS, 2 * ROWS)] = (scale * value).astype(jnp.bfloat16)

    def text_rows(group):
        rows = pl.ds(group * ROWS, ROWS)
        text_part[rows, :] = jnp.dot(coef[rows, :], images[...], preferred_element_type=jnp.float32)

    def image_rows(pair):
        lanes = pl.ds(pair * 2 * ROWS, 2 * ROWS)
        image_part[lanes, :] = lax.dot_general(coef[:, lanes], texts[...], TN, preferred_element_type=jnp.float32)

    def pack_text(row, rows):
        text_send[pl.ds(row - ROWS, rows), :] = packed(text_part[pl.ds(row, rows), :])

    load_text.wait()
    texts[pl.ds(0, ROWS), :] = text_in[...].astype(jnp.bfloat16)
    pl.semaphore_wait(barrier, 5)
    y_near = []
    for i in range(2):
        y_near.append((
            send(right, texts, PIECE * i, texts, 320 + PIECE * i, PIECE),
            send(left, texts, HALF + PIECE * i, texts, 480 + PIECE * i, PIECE),
        ))
    load_image.wait()
    images[pl.ds(0, ROWS), :] = image_in[...].astype(jnp.bfloat16)
    z_image = [send(partner, images, PIECE * i, images, 640 + PIECE * i, PIECE) for i in range(4)]
    n_image = send(before, images, 0, images, 320, ROWS)

    y_far, nz_image = [], []

    def forward_y(i):
        y_near[i][0].wait_recv()
        a = send(right, texts, 320 + PIECE * i, texts, 640 + PIECE * i, PIECE)
        y_near[i][1].wait_recv()
        b = send(left, texts, 480 + PIECE * i, texts, 800 + PIECE * i, PIECE)
        y_far.append((a, b))

    def forward_z(i):
        z_image[i].wait_recv()
        nz_image.append(send(before, images, 640 + PIECE * i, images, 960 + PIECE * i, PIECE))

    forward_y(0)
    forward_z(0)
    forward_y(1)
    y_last = (send(right, texts, HALF, texts, 960, HALF), send(left, texts, 0, texts, 1120, HALF))
    forward_z(1)
    n_image.wait_recv()
    coefficients(0, 0)
    coefficients(1, 0)
    forward_z(2)
    for i in range(2):
        for copy in y_far[i]:
            copy.wait_recv()
    forward_z(3)
    coefficients(2, 0)
    for copy in nz_image:
        copy.wait_recv()

    coefficients(1, 1)
    text_rows(1)
    pack_text(320, ROWS)
    near = [(send(left, text_send, 0, right_recv, 0, PIECE), send(right, text_send, 160, left_recv, 160, PIECE))]
    coefficients(2, 1)
    text_rows(2)
    pack_text(640, ROWS)
    mid = []
    for i in range(2):
        mid.append((
            send(left, text_send, 480 + PIECE * i, mid_recv, PIECE * i, PIECE),
            send(right, text_send, 320 + PIECE * i, mid_recv, HALF + PIECE * i, PIECE),
        ))
    near.append((send(left, text_send, PIECE, right_recv, PIECE, PIECE), send(right, text_send, 240, left_recv, 240, PIECE)))
    coefficients(0, 1)
    for copy in y_last:
        copy.wait_recv()
    coefficients(3, 1)
    coefficients(3, 0)
    image_rows(1)
    image_send[pl.ds(640, ROWS), :] = packed(image_part[pl.ds(960, ROWS), :])
    nz_part = [send(after, image_send, 640 + PIECE * i, zn_recv, PIECE * i, PIECE) for i in range(4)]
    image_rows(0)
    image_send[pl.ds(0, ROWS), :] = packed(image_part[pl.ds(320, ROWS), :])
    n_part = send(after, image_send, 0, dn_recv, 0, ROWS)
    text_rows(3)
    text_rows(0)

    z_part, last = [], []

    def reduce_z(i):
        nz_part[i].wait_recv()
        rows = pl.ds(PIECE * i, PIECE)
        image_send[pl.ds(320 + PIECE * i, PIECE), :] = packed(
            image_part[pl.ds(640 + PIECE * i, PIECE), :] + unpacked(zn_recv[rows, :])
        )
        z_part.append(send(partner, image_send, 320 + PIECE * i, z_recv, PIECE * i, PIECE))

    def reduce_y(i):
        pair = []
        for k, device, target, target_row in ((0, left, right_recv, HALF), (1, right, left_recv, 0)):
            mid[i][k].wait_recv()
            row = HALF * k + PIECE * i
            text_send[pl.ds(640 + row, PIECE), :] = packed(
                text_part[pl.ds(960 + row, PIECE), :] + unpacked(mid_recv[pl.ds(row, PIECE), :])
            )
            pair.append(send(device, text_send, 640 + row, target, target_row + PIECE * i, PIECE))
        last.append(pair)

    reduce_z(0)
    reduce_z(1)
    reduce_y(0)
    reduce_z(2)
    reduce_z(3)
    reduce_y(1)

    n_part.wait_recv()
    image_sum[...] = image_part[pl.ds(0, ROWS), :] + unpacked(dn_recv[...])
    stores = []

    def store(source, target, row, rows):
        copy = pltpu.make_async_copy(
            source.at[pl.ds(row, rows)], target.at[pl.ds(row, rows)], store_sem.at[len(stores)]
        )
        copy.start()
        stores.append(copy)

    for i in range(2):
        for j in (2 * i, 2 * i + 1):
            z_part[j].wait_recv()
        rows = pl.ds(HALF * i, HALF)
        image_sum[rows, :] += unpacked(z_recv[rows, :])
        store(image_sum, image_out, HALF * i, HALF)
    for pair in near:
        for copy in pair:
            copy.wait_recv()
    text_sum[pl.ds(0, HALF), :] = text_part[pl.ds(0, HALF), :] + unpacked(right_recv[pl.ds(0, HALF), :])
    text_sum[pl.ds(HALF, HALF), :] = text_part[pl.ds(HALF, HALF), :] + unpacked(left_recv[pl.ds(HALF, HALF), :])
    for i in range(2):
        for k, source, row in ((0, right_recv, HALF), (1, left_recv, 0)):
            last[i][k].wait_recv()
            rows = pl.ds(row + PIECE * i, PIECE)
            text_sum[rows, :] += unpacked(source[rows, :])
            store(text_sum, text_out, row + PIECE * i, PIECE)
    for copy in copies:
        copy.wait_send()
    for copy in stores:
        copy.wait()


def per_device(image_embed, text_embed, logit_scale, logit_bias):
    half = lambda rows: pltpu.VMEM((rows, WIDTH), jnp.bfloat16)
    full = lambda rows: pltpu.VMEM((rows, WIDTH), jnp.float32)
    n_copies = 48
    out = jax.ShapeDtypeStruct((ROWS, WIDTH), jnp.float32)
    return pl.pallas_call(
        kernel,
        out_shape=(out, out),
        in_specs=[pl.BlockSpec(memory_space=pltpu.SMEM)] * 2 + [pl.BlockSpec(memory_space=pl.ANY)] * 2,
        out_specs=(pl.BlockSpec(memory_space=pl.ANY),) * 2,
        scratch_shapes=[
            full(ROWS), full(ROWS), half(BLOCK), half(BLOCK), pltpu.VMEM((BLOCK, BLOCK), jnp.bfloat16),
            full(BLOCK), full(BLOCK),
            half(3 * ROWS), half(3 * ROWS), half(ROWS), half(ROWS), half(ROWS), half(ROWS), half(ROWS), half(ROWS),
            full(ROWS), full(ROWS),
            pltpu.SemaphoreType.DMA((2,)), pltpu.SemaphoreType.DMA((6,)),
            pltpu.SemaphoreType.DMA((n_copies,)), pltpu.SemaphoreType.DMA((n_copies,)),
        ],
        compiler_params=pltpu.CompilerParams(
            collective_id=0, has_side_effects=True, vmem_limit_bytes=60 * 2**20
        ),
        cost_estimate=pl.CostEstimate(
            flops=6 * BLOCK * BLOCK * WIDTH, bytes_accessed=16 * ROWS * WIDTH, transcendentals=BLOCK * BLOCK
        ),
    )(logit_scale.reshape(1), logit_bias.reshape(1), image_embed, text_embed)


def solution(mesh):
    placed = (P(("node", "local"), None), P(("node", "local"), None), P(), P())
    return jax.shard_map(
        per_device,
        mesh=mesh,
        in_specs=placed,
        out_specs=(P(("node", "local"), None), P(("node", "local"), None)),
        check_vma=False,
    )
```

```python
import jax
import jax.numpy as jnp
from jax import lax
from jax.experimental import pallas as pl
from jax.experimental.pallas import tpu as pltpu
from jax.sharding import PartitionSpec as P

MESH = pl.DeviceIdType.MESH
ROWS, WIDTH = 320, 1152
HALF, PIECE = ROWS // 2, ROWS // 4
BLOCK = 4 * ROWS
NT = (((1,), (1,)), ((), ()))
TN = (((0,), (0,)), ((), ()))


def neighbours():
    node, local = lax.axis_index("node"), lax.axis_index("local")
    z_hi, x, core = node // 8, (node // 2) % 4, node % 2
    z_lo, y = local // 4, local % 4
    right = (node, z_lo * 4 + (y + 1) % 4)
    left = (node, z_lo * 4 + (y + 3) % 4)
    partner = (node, (1 - z_lo) * 4 + y)
    first = jnp.logical_and(core == 0, x == 0)
    last = jnp.logical_and(core == 1, x == 3)
    flipped = (1 - z_lo) * 4 + y
    before = ((node + 15) % 16, jnp.where(first, flipped, local))
    after = ((node + 1) % 16, jnp.where(last, flipped, local))
    return right, left, partner, before, after


def packed(value):
    square = value * value
    return (square * (value * jnp.abs(value))).astype(jnp.bfloat16)


def unpacked(power):
    power = power.astype(jnp.float32)
    root = lax.rsqrt(jnp.maximum(jnp.abs(power), 1e-37))
    return (power * root) * (root * lax.rsqrt(root))


def kernel(
    scale_ref, bias_ref, image_hbm, text_hbm, image_out, text_out,
    image_in, text_in, texts, images, coef, text_part, image_part,
    text_send, image_send, mid_recv, right_recv, left_recv, zn_recv, dn_recv, z_recv,
    load_sem, send_sem, recv_sem,
):
    right, left, partner, before, after = neighbours()
    core = lax.axis_index("node") % 2
    scale, bias = scale_ref[0], bias_ref[0]
    load_text = pltpu.make_async_copy(text_hbm, text_in, load_sem.at[0])
    load_image = pltpu.make_async_copy(image_hbm, image_in, load_sem.at[1])
    load_text.start()
    load_image.start()
    barrier = pltpu.get_barrier_semaphore()
    for device in (right, left, partner, before, after):
        pl.semaphore_signal(barrier, 1, device_id=device, device_id_type=MESH)

    copies = []

    def send(device, source, source_row, target, target_row, rows, start=True):
        k = len(copies)
        copy = pltpu.make_async_remote_copy(
            src_ref=source.at[pl.ds(source_row, rows)],
            dst_ref=target.at[pl.ds(target_row, rows)],
            send_sem=send_sem.at[k],
            recv_sem=recv_sem.at[k],
            device_id=device,
            device_id_type=MESH,
        )
        copies.append(copy)
        if start:
            copy.start()
        return copy

    def coefficients(group, pair):
        block = texts[pl.ds(group * ROWS, ROWS), :]
        logits = scale * lax.dot_general(
            block, images[pl.ds(pair * 2 * ROWS, 2 * ROWS), :], NT, preferred_element_type=jnp.float32
        ) + bias
        value = 1.0 / (1.0 + jnp.exp(-logits))
        if group == 0 and pair == 0:
            shape = (ROWS, 2 * ROWS)
            match = lax.broadcasted_iota(jnp.int32, shape, 0) == lax.broadcasted_iota(jnp.int32, shape, 1)
            value = value - match.astype(jnp.float32)
        coef[pl.ds(group * ROWS, ROWS), pl.ds(pair * 2 * ROWS, 2 * ROWS)] = (scale * value).astype(jnp.bfloat16)

    def text_rows(group):
        rows = pl.ds(group * ROWS, ROWS)
        text_part[rows, :] = jnp.dot(coef[rows, :], images[...], preferred_element_type=jnp.float32)

    def image_rows(pair, first, rows):
        lanes = pl.ds(pair * 2 * ROWS, 2 * ROWS)
        part = lax.dot_general(
            coef[pl.ds(first, rows), lanes], texts[pl.ds(first, rows), :], TN, preferred_element_type=jnp.float32
        )
        if first:
            image_part[lanes, :] += part
        else:
            image_part[lanes, :] = part

    def pack_text(row, rows):
        text_send[pl.ds(row - ROWS, rows), :] = packed(text_part[pl.ds(row, rows), :])

    load_text.wait()
    texts[pl.ds(0, ROWS), :] = text_in[...].astype(jnp.bfloat16)
    load_image.wait()
    images[pl.ds(0, ROWS), :] = image_in[...].astype(jnp.bfloat16)
    pl.semaphore_wait(barrier, 5)
    y_near = []
    for i in range(2):
        y_near.append((
            send(right, texts, PIECE * i, texts, 320 + PIECE * i, PIECE),
            send(left, texts, HALF + PIECE * i, texts, 480 + PIECE * i, PIECE),
        ))
    z_image = [send(partner, images, PIECE * i, images, 640 + PIECE * i, PIECE, False) for i in range(4)]
    nz_image = [send(before, images, 640 + PIECE * i, images, 960 + PIECE * i, PIECE, False) for i in range(4)]

    def start_z(which):
        @pl.when(core == which)
        def _():
            for copy in z_image:
                copy.start()

    def forward_z(which, pieces):
        @pl.when(core == which)
        def _():
            for i in pieces:
                z_image[i].wait_recv()
                nz_image[i].start()

    start_z(0)
    n_image = send(before, images, 0, images, 320, ROWS)
    y_far = []

    def forward_y(i):
        y_near[i][0].wait_recv()
        a = send(right, texts, 320 + PIECE * i, texts, 640 + PIECE * i, PIECE)
        y_near[i][1].wait_recv()
        b = send(left, texts, 480 + PIECE * i, texts, 800 + PIECE * i, PIECE)
        y_far.append((a, b))

    forward_y(0)
    start_z(1)
    forward_z(0, (0, 1))
    forward_y(1)
    y_last = (send(right, texts, HALF, texts, 960, HALF), send(left, texts, 0, texts, 1120, HALF))
    forward_z(0, (2, 3))
    n_image.wait_recv()
    coefficients(0, 0)
    forward_z(1, (0,))
    coefficients(1, 0)
    forward_z(1, (1, 2))
    for copy in y_far[0]:
        copy.wait_recv()
    forward_z(1, (3,))
    for copy in y_far[1]:
        copy.wait_recv()
    coefficients(2, 0)
    for copy in nz_image:
        copy.wait_recv()

    coefficients(1, 1)
    text_rows(1)
    pack_text(320, ROWS)
    near = [(send(left, text_send, 0, right_recv, 0, PIECE), send(right, text_send, 160, left_recv, 160, PIECE))]
    coefficients(2, 1)
    text_rows(2)
    pack_text(640, ROWS)
    mid = []
    for i in range(2):
        mid.append((
            send(left, text_send, 480 + PIECE * i, mid_recv, PIECE * i, PIECE),
            send(right, text_send, 320 + PIECE * i, mid_recv, HALF + PIECE * i, PIECE),
        ))
    near.append((send(left, text_send, PIECE, right_recv, PIECE, PIECE), send(right, text_send, 240, left_recv, 240, PIECE)))
    coefficients(0, 1)
    image_rows(1, 0, 3 * ROWS)
    for copy in y_last:
        copy.wait_recv()
    coefficients(3, 1)
    image_rows(1, 3 * ROWS, ROWS)
    image_send[pl.ds(640, ROWS), :] = packed(image_part[pl.ds(960, ROWS), :])
    nz_part = [send(after, image_send, 640 + PIECE * i, zn_recv, PIECE * i, PIECE) for i in range(4)]
    coefficients(3, 0)
    image_rows(0, 0, BLOCK)
    image_send[pl.ds(0, ROWS), :] = packed(image_part[pl.ds(320, ROWS), :])
    n_part = send(after, image_send, 0, dn_recv, 0, ROWS)
    text_rows(3)
    text_rows(0)

    z_part, last = [], []

    def reduce_z(i):
        nz_part[i].wait_recv()
        rows = pl.ds(PIECE * i, PIECE)
        image_send[pl.ds(320 + PIECE * i, PIECE), :] = packed(
            image_part[pl.ds(640 + PIECE * i, PIECE), :] + unpacked(zn_recv[rows, :])
        )
        z_part.append(send(partner, image_send, 320 + PIECE * i, z_recv, PIECE * i, PIECE))

    def reduce_y(i):
        pair = []
        for k, device, target, target_row in ((0, left, right_recv, HALF), (1, right, left_recv, 0)):
            mid[i][k].wait_recv()
            row = HALF * k + PIECE * i
            text_send[pl.ds(640 + row, PIECE), :] = packed(
                text_part[pl.ds(960 + row, PIECE), :] + unpacked(mid_recv[pl.ds(row, PIECE), :])
            )
            pair.append(send(device, text_send, 640 + row, target, target_row + PIECE * i, PIECE))
        last.append(pair)

    reduce_z(0)
    reduce_z(1)
    reduce_y(0)
    reduce_z(2)
    reduce_z(3)
    reduce_y(1)

    n_part.wait_recv()
    image_out[...] = image_part[pl.ds(0, ROWS), :] + unpacked(dn_recv[...])
    for i in range(2):
        for j in (2 * i, 2 * i + 1):
            z_part[j].wait_recv()
        rows = pl.ds(HALF * i, HALF)
        image_out[rows, :] += unpacked(z_recv[rows, :])
    for pair in near:
        for copy in pair:
            copy.wait_recv()
    text_out[pl.ds(0, HALF), :] = text_part[pl.ds(0, HALF), :] + unpacked(right_recv[pl.ds(0, HALF), :])
    text_out[pl.ds(HALF, HALF), :] = text_part[pl.ds(HALF, HALF), :] + unpacked(left_recv[pl.ds(HALF, HALF), :])
    for i in range(2):
        for k, source, row in ((0, right_recv, HALF), (1, left_recv, 0)):
            last[i][k].wait_recv()
            rows = pl.ds(row + PIECE * i, PIECE)
            text_out[rows, :] += unpacked(source[rows, :])
    for copy in copies:
        copy.wait_send()


def per_device(image_embed, text_embed, logit_scale, logit_bias):
    half = lambda rows: pltpu.VMEM((rows, WIDTH), jnp.bfloat16)
    full = lambda rows: pltpu.VMEM((rows, WIDTH), jnp.float32)
    n_copies = 48
    out = pltpu.VMEM((ROWS, WIDTH), jnp.float32)
    return pl.pallas_call(
        kernel,
        out_shape=(out, out),
        in_specs=[pl.BlockSpec(memory_space=pltpu.SMEM)] * 2 + [pl.BlockSpec(memory_space=pltpu.HBM)] * 2,
        out_specs=(pl.BlockSpec(memory_space=pltpu.VMEM),) * 2,
        scratch_shapes=[
            full(ROWS), full(ROWS), half(BLOCK), half(BLOCK), pltpu.VMEM((BLOCK, BLOCK), jnp.bfloat16),
            full(BLOCK), full(BLOCK),
            half(3 * ROWS), half(3 * ROWS), half(ROWS), half(ROWS), half(ROWS), half(ROWS), half(ROWS), half(ROWS),
            pltpu.SemaphoreType.DMA((2,)),
            pltpu.SemaphoreType.DMA((n_copies,)), pltpu.SemaphoreType.DMA((n_copies,)),
        ],
        compiler_params=pltpu.CompilerParams(
            collective_id=0, has_side_effects=True, vmem_limit_bytes=60 * 2**20
        ),
        cost_estimate=pl.CostEstimate(
            flops=6 * BLOCK * BLOCK * WIDTH, bytes_accessed=16 * ROWS * WIDTH, transcendentals=BLOCK * BLOCK
        ),
    )(logit_scale.reshape(1), logit_bias.reshape(1), image_embed, text_embed)


def solution(mesh):
    placed = (P(("node", "local"), None), P(("node", "local"), None), P(), P())
    return jax.shard_map(
        per_device,
        mesh=mesh,
        in_specs=placed,
        out_specs=(P(("node", "local"), None), P(("node", "local"), None)),
        check_vma=False,
    )
```

```python
import jax
import jax.numpy as jnp
from jax import lax
from jax.experimental import pallas as pl
from jax.experimental.pallas import tpu as pltpu
from jax.sharding import PartitionSpec as P

MESH = pl.DeviceIdType.MESH
ROWS, WIDTH = 320, 1152
HALF, PIECE = ROWS // 2, ROWS // 4
BLOCK = 4 * ROWS
NT = (((1,), (1,)), ((), ()))
TN = (((0,), (0,)), ((), ()))


def neighbours():
    node, local = lax.axis_index("node"), lax.axis_index("local")
    z_hi, x, core = node // 8, (node // 2) % 4, node % 2
    z_lo, y = local // 4, local % 4
    right = (node, z_lo * 4 + (y + 1) % 4)
    left = (node, z_lo * 4 + (y + 3) % 4)
    partner = (node, (1 - z_lo) * 4 + y)
    first = jnp.logical_and(core == 0, x == 0)
    last = jnp.logical_and(core == 1, x == 3)
    flipped = (1 - z_lo) * 4 + y
    before = ((node + 15) % 16, jnp.where(first, flipped, local))
    after = ((node + 1) % 16, jnp.where(last, flipped, local))
    return right, left, partner, before, after


def packed(value):
    square = value * value
    return (square * (value * jnp.abs(value))).astype(jnp.bfloat16)


def unpacked(power):
    power = power.astype(jnp.float32)
    root = lax.rsqrt(jnp.maximum(jnp.abs(power), 1e-37))
    return (power * root) * (root * lax.rsqrt(root))


def kernel(
    scale_ref, bias_ref, image_hbm, text_hbm, image_out, text_out,
    image_in, text_in, texts, images, coef, text_part, image_part,
    text_send, image_send, mid_recv, right_recv, left_recv, zn_recv, dn_recv, z_recv,
    load_sem, send_sem, recv_sem,
):
    right, left, partner, before, after = neighbours()
    core = lax.axis_index("node") % 2
    scale, bias = scale_ref[0], bias_ref[0]
    load_text = pltpu.make_async_copy(text_hbm, text_in, load_sem.at[0])
    load_image = pltpu.make_async_copy(image_hbm, image_in, load_sem.at[1])
    load_text.start()
    load_image.start()
    barrier = pltpu.get_barrier_semaphore()
    for device in (right, left, partner, before, after):
        pl.semaphore_signal(barrier, 1, device_id=device, device_id_type=MESH)

    copies = []

    def send(device, source, source_row, target, target_row, rows, start=True):
        k = len(copies)
        copy = pltpu.make_async_remote_copy(
            src_ref=source.at[pl.ds(source_row, rows)],
            dst_ref=target.at[pl.ds(target_row, rows)],
            send_sem=send_sem.at[k],
            recv_sem=recv_sem.at[k],
            device_id=device,
            device_id_type=MESH,
        )
        copies.append(copy)
        if start:
            copy.start()
        return copy

    def coefficients(group, lane, lanes):
        rows, place = pl.ds(group * ROWS, ROWS), pl.ds(lane, lanes)
        logits = scale * lax.dot_general(
            texts[rows, :], images[place, :], NT, preferred_element_type=jnp.float32
        ) + bias
        value = 1.0 / (1.0 + jnp.exp(-logits))
        if group == 0 and lane == 0:
            shape = (ROWS, lanes)
            match = lax.broadcasted_iota(jnp.int32, shape, 0) == lax.broadcasted_iota(jnp.int32, shape, 1)
            value = value - match.astype(jnp.float32)
        coef[rows, place] = (scale * value).astype(jnp.bfloat16)

    def text_rows(group, pair):
        rows, lanes = pl.ds(group * ROWS, ROWS), pl.ds(pair * 2 * ROWS, 2 * ROWS)
        part = jnp.dot(coef[rows, lanes], images[lanes, :], preferred_element_type=jnp.float32)
        if pair:
            part = text_part[rows, :] + part
        text_part[rows, :] = part

    def image_rows(lane, lanes, first, rows):
        place = pl.ds(lane, lanes)
        part = lax.dot_general(
            coef[pl.ds(first, rows), place], texts[pl.ds(first, rows), :], TN, preferred_element_type=jnp.float32
        )
        if first:
            part = image_part[place, :] + part
        image_part[place, :] = part

    def pack_text(row, rows):
        text_send[pl.ds(row - ROWS, rows), :] = packed(text_part[pl.ds(row, rows), :])

    load_text.wait()
    texts[pl.ds(0, ROWS), :] = text_in[...].astype(jnp.bfloat16)
    load_image.wait()
    images[pl.ds(0, ROWS), :] = image_in[...].astype(jnp.bfloat16)
    pl.semaphore_wait(barrier, 5)
    y_near = []
    for i in range(2):
        y_near.append((
            send(right, texts, PIECE * i, texts, 320 + PIECE * i, PIECE),
            send(left, texts, HALF + PIECE * i, texts, 480 + PIECE * i, PIECE),
        ))
    z_image = [send(partner, images, PIECE * i, images, 640 + PIECE * i, PIECE, False) for i in range(4)]
    nz_image = [send(before, images, 640 + PIECE * i, images, 960 + PIECE * i, PIECE, False) for i in range(4)]

    def start_z(which):
        @pl.when(core == which)
        def _():
            for copy in z_image:
                copy.start()

    def forward_z(which, pieces):
        @pl.when(core == which)
        def _():
            for i in pieces:
                z_image[i].wait_recv()
                nz_image[i].start()

    start_z(0)
    n_image = send(before, images, 0, images, 320, ROWS)
    y_far = []

    def forward_y(i):
        y_near[i][0].wait_recv()
        a = send(right, texts, 320 + PIECE * i, texts, 640 + PIECE * i, PIECE)
        y_near[i][1].wait_recv()
        b = send(left, texts, 480 + PIECE * i, texts, 800 + PIECE * i, PIECE)
        y_far.append((a, b))

    forward_y(0)
    start_z(1)
    forward_z(0, (0, 1))
    forward_y(1)
    y_last = (send(right, texts, HALF, texts, 960, HALF), send(left, texts, 0, texts, 1120, HALF))
    n_image.wait_recv()
    coefficients(0, 0, 640)
    coefficients(1, 0, 640)
    forward_z(0, (2,))
    forward_z(1, (0, 1))
    text_rows(1, 0)
    text_rows(0, 0)
    image_rows(0, 640, 0, 2 * ROWS)
    forward_z(0, (3,))
    forward_z(1, (2, 3))
    coefficients(1, 640, 256)
    coefficients(0, 640, 256)
    for i in range(2):
        for copy in y_far[i]:
            copy.wait_recv()
    coefficients(2, 0, 640)
    coefficients(2, 640, 256)
    for copy in nz_image:
        copy.wait_recv()

    coefficients(1, 896, 384)
    text_rows(1, 1)
    pack_text(320, ROWS)
    near = [
        (
            send(left, text_send, PIECE * i, right_recv, PIECE * i, PIECE),
            send(right, text_send, HALF + PIECE * i, left_recv, HALF + PIECE * i, PIECE),
        )
        for i in range(2)
    ]
    coefficients(2, 896, 384)
    coefficients(0, 896, 384)
    image_rows(896, 384, 0, 3 * ROWS)
    image_rows(640, 256, 0, 3 * ROWS)
    for copy in y_last:
        copy.wait_recv()
    coefficients(3, 640, 640)
    image_rows(896, 384, 3 * ROWS, ROWS)
    image_send[pl.ds(640, ROWS), :] = packed(image_part[pl.ds(960, ROWS), :])
    nz_part = [send(after, image_send, 640 + PIECE * i, zn_recv, PIECE * i, PIECE) for i in range(4)]
    image_rows(640, 256, 3 * ROWS, ROWS)
    text_rows(2, 0)
    text_rows(2, 1)
    pack_text(640, ROWS)
    mid = []
    for i in range(2):
        mid.append((
            send(left, text_send, 480 + PIECE * i, mid_recv, PIECE * i, PIECE),
            send(right, text_send, 320 + PIECE * i, mid_recv, HALF + PIECE * i, PIECE),
        ))
    z_part = [send(partner, image_send, 320 + PIECE * i, z_recv, PIECE * i, PIECE, False) for i in range(4)]
    last = []

    def reduce_z(which, pieces):
        @pl.when(core == which)
        def _():
            for i in pieces:
                nz_part[i].wait_recv()
                rows = pl.ds(PIECE * i, PIECE)
                image_send[pl.ds(320 + PIECE * i, PIECE), :] = packed(
                    image_part[pl.ds(640 + PIECE * i, PIECE), :] + unpacked(zn_recv[rows, :])
                )
                z_part[i].start()

    def reduce_y(i):
        pair = []
        for k, device, target, target_row in ((0, left, right_recv, HALF), (1, right, left_recv, 0)):
            mid[i][k].wait_recv()
            row = HALF * k + PIECE * i
            text_send[pl.ds(640 + row, PIECE), :] = packed(
                text_part[pl.ds(960 + row, PIECE), :] + unpacked(mid_recv[pl.ds(row, PIECE), :])
            )
            pair.append(send(device, text_send, 640 + row, target, target_row + PIECE * i, PIECE))
        last.append(pair)

    reduce_z(1, range(4))
    coefficients(3, 0, 640)
    image_rows(0, 640, 2 * ROWS, 2 * ROWS)
    image_send[pl.ds(0, ROWS), :] = packed(image_part[pl.ds(320, ROWS), :])
    n_part = send(after, image_send, 0, dn_recv, 0, ROWS)
    reduce_z(0, (0,))
    text_rows(3, 0)
    text_rows(3, 1)
    reduce_z(0, (1,))
    text_rows(0, 1)
    reduce_z(0, (2, 3))
    reduce_y(0)
    reduce_y(1)

    n_part.wait_recv()
    image_out[...] = image_part[pl.ds(0, ROWS), :] + unpacked(dn_recv[...])
    for i in range(2):
        for j in (2 * i, 2 * i + 1):
            z_part[j].wait_recv()
        rows = pl.ds(HALF * i, HALF)
        image_out[rows, :] += unpacked(z_recv[rows, :])
    for pair in near:
        for copy in pair:
            copy.wait_recv()
    text_out[pl.ds(0, HALF), :] = text_part[pl.ds(0, HALF), :] + unpacked(right_recv[pl.ds(0, HALF), :])
    text_out[pl.ds(HALF, HALF), :] = text_part[pl.ds(HALF, HALF), :] + unpacked(left_recv[pl.ds(HALF, HALF), :])
    for i in range(2):
        for k, source, row in ((0, right_recv, HALF), (1, left_recv, 0)):
            last[i][k].wait_recv()
            rows = pl.ds(row + PIECE * i, PIECE)
            text_out[rows, :] += unpacked(source[rows, :])
    for copy in copies:
        copy.wait_send()


def per_device(image_embed, text_embed, logit_scale, logit_bias):
    half = lambda rows: pltpu.VMEM((rows, WIDTH), jnp.bfloat16)
    full = lambda rows: pltpu.VMEM((rows, WIDTH), jnp.float32)
    n_copies = 48
    out = pltpu.VMEM((ROWS, WIDTH), jnp.float32)
    return pl.pallas_call(
        kernel,
        out_shape=(out, out),
        in_specs=[pl.BlockSpec(memory_space=pltpu.SMEM)] * 2 + [pl.BlockSpec(memory_space=pltpu.HBM)] * 2,
        out_specs=(pl.BlockSpec(memory_space=pltpu.VMEM),) * 2,
        scratch_shapes=[
            full(ROWS), full(ROWS), half(BLOCK), half(BLOCK), pltpu.VMEM((BLOCK, BLOCK), jnp.bfloat16),
            full(BLOCK), full(BLOCK),
            half(3 * ROWS), half(3 * ROWS), half(ROWS), half(ROWS), half(ROWS), half(ROWS), half(ROWS), half(ROWS),
            pltpu.SemaphoreType.DMA((2,)),
            pltpu.SemaphoreType.DMA((n_copies,)), pltpu.SemaphoreType.DMA((n_copies,)),
        ],
        compiler_params=pltpu.CompilerParams(
            collective_id=0, has_side_effects=True, vmem_limit_bytes=60 * 2**20
        ),
        cost_estimate=pl.CostEstimate(
            flops=6 * BLOCK * BLOCK * WIDTH, bytes_accessed=16 * ROWS * WIDTH, transcendentals=BLOCK * BLOCK
        ),
    )(logit_scale.reshape(1), logit_bias.reshape(1), image_embed, text_embed)


def solution(mesh):
    placed = (P(("node", "local"), None), P(("node", "local"), None), P(), P())
    return jax.shard_map(
        per_device,
        mesh=mesh,
        in_specs=placed,
        out_specs=(P(("node", "local"), None), P(("node", "local"), None)),
        check_vma=False,
    )
```

```python
import jax
import jax.numpy as jnp
from jax import lax
from jax.experimental import pallas as pl
from jax.experimental.pallas import tpu as pltpu
from jax.sharding import PartitionSpec as P

MESH = pl.DeviceIdType.MESH
ROWS, WIDTH = 320, 1152
HALF, PIECE = ROWS // 2, ROWS // 4
BLOCK = 4 * ROWS
NT = (((1,), (1,)), ((), ()))
TN = (((0,), (0,)), ((), ()))


def neighbours():
    node, local = lax.axis_index("node"), lax.axis_index("local")
    z_hi, x, core = node // 8, (node // 2) % 4, node % 2
    z_lo, y = local // 4, local % 4
    right = (node, z_lo * 4 + (y + 1) % 4)
    left = (node, z_lo * 4 + (y + 3) % 4)
    partner = (node, (1 - z_lo) * 4 + y)
    first = jnp.logical_and(core == 0, x == 0)
    last = jnp.logical_and(core == 1, x == 3)
    flipped = (1 - z_lo) * 4 + y
    before = ((node + 15) % 16, jnp.where(first, flipped, local))
    after = ((node + 1) % 16, jnp.where(last, flipped, local))
    return right, left, partner, before, after


def packed(value):
    square = value * value
    return (square * (value * jnp.abs(value))).astype(jnp.bfloat16)


def unpacked(power):
    power = power.astype(jnp.float32)
    root = lax.rsqrt(jnp.maximum(jnp.abs(power), 1e-37))
    return (power * root) * (root * lax.rsqrt(root))


def kernel(
    scale_ref, bias_ref, image_hbm, text_hbm, image_out, text_out,
    image_in, text_in, texts, images, coef, text_part, image_part,
    text_send, image_send, mid_recv, right_recv, left_recv, zn_recv, dn_recv, z_recv,
    load_sem, send_sem, recv_sem,
):
    right, left, partner, before, after = neighbours()
    core = lax.axis_index("node") % 2
    scale, bias = scale_ref[0], bias_ref[0]
    load_text = pltpu.make_async_copy(text_hbm, text_in, load_sem.at[0])
    load_image = pltpu.make_async_copy(image_hbm, image_in, load_sem.at[1])
    load_text.start()
    load_image.start()
    barrier = pltpu.get_barrier_semaphore()
    for device in (right, left, partner, before, after):
        pl.semaphore_signal(barrier, 1, device_id=device, device_id_type=MESH)

    copies = []

    def send(device, source, source_row, target, target_row, rows, start=True):
        k = len(copies)
        copy = pltpu.make_async_remote_copy(
            src_ref=source.at[pl.ds(source_row, rows)],
            dst_ref=target.at[pl.ds(target_row, rows)],
            send_sem=send_sem.at[k],
            recv_sem=recv_sem.at[k],
            device_id=device,
            device_id_type=MESH,
        )
        copies.append(copy)
        if start:
            copy.start()
        return copy

    def coefficients(group, lane, lanes):
        rows, place = pl.ds(group * ROWS, ROWS), pl.ds(lane, lanes)
        logits = scale * lax.dot_general(
            texts[rows, :], images[place, :], NT, preferred_element_type=jnp.float32
        ) + bias
        value = 1.0 / (1.0 + jnp.exp(-logits))
        if group == 0 and lane == 0:
            shape = (ROWS, lanes)
            match = lax.broadcasted_iota(jnp.int32, shape, 0) == lax.broadcasted_iota(jnp.int32, shape, 1)
            value = value - match.astype(jnp.float32)
        coef[rows, place] = (scale * value).astype(jnp.bfloat16)

    def text_rows(group, pair):
        rows, lanes = pl.ds(group * ROWS, ROWS), pl.ds(pair * 2 * ROWS, 2 * ROWS)
        part = jnp.dot(coef[rows, lanes], images[lanes, :], preferred_element_type=jnp.float32)
        if pair:
            part = text_part[rows, :] + part
        text_part[rows, :] = part

    def image_rows(lane, lanes, first, rows):
        place = pl.ds(lane, lanes)
        part = lax.dot_general(
            coef[pl.ds(first, rows), place], texts[pl.ds(first, rows), :], TN, preferred_element_type=jnp.float32
        )
        if first:
            part = image_part[place, :] + part
        image_part[place, :] = part

    def pack_text(row, rows):
        text_send[pl.ds(row - ROWS, rows), :] = packed(text_part[pl.ds(row, rows), :])

    load_text.wait()
    texts[pl.ds(0, ROWS), :] = text_in[...].astype(jnp.bfloat16)
    load_image.wait()
    images[pl.ds(0, ROWS), :] = image_in[...].astype(jnp.bfloat16)
    pl.semaphore_wait(barrier, 5)
    y_near = []
    for i in range(2):
        y_near.append((
            send(right, texts, PIECE * i, texts, 320 + PIECE * i, PIECE),
            send(left, texts, HALF + PIECE * i, texts, 480 + PIECE * i, PIECE),
        ))
    z_image = [send(partner, images, PIECE * i, images, 640 + PIECE * i, PIECE, False) for i in range(4)]
    nz_image = [send(before, images, 640 + PIECE * i, images, 960 + PIECE * i, PIECE, False) for i in range(4)]

    def start_z(which):
        @pl.when(core == which)
        def _():
            for copy in z_image:
                copy.start()

    def forward_z(which, pieces):
        @pl.when(core == which)
        def _():
            for i in pieces:
                z_image[i].wait_recv()
                nz_image[i].start()

    start_z(0)
    n_image = send(before, images, 0, images, 320, ROWS)
    y_far = []

    def forward_y(i):
        y_near[i][0].wait_recv()
        a = send(right, texts, 320 + PIECE * i, texts, 640 + PIECE * i, PIECE)
        y_near[i][1].wait_recv()
        b = send(left, texts, 480 + PIECE * i, texts, 800 + PIECE * i, PIECE)
        y_far.append((a, b))

    forward_y(0)
    start_z(1)
    forward_z(0, (0, 1))
    forward_y(1)
    y_last = (send(right, texts, HALF, texts, 960, HALF), send(left, texts, 0, texts, 1120, HALF))
    n_image.wait_recv()
    coefficients(0, 0, 640)
    coefficients(1, 0, 640)
    forward_z(0, (2,))
    forward_z(1, (0, 1))
    text_rows(1, 0)
    text_rows(0, 0)
    image_rows(0, 640, 0, 2 * ROWS)
    forward_z(0, (3,))
    forward_z(1, (2, 3))
    coefficients(1, 640, 256)
    coefficients(0, 640, 256)
    for i in range(2):
        for copy in y_far[i]:
            copy.wait_recv()
    coefficients(2, 0, 640)
    coefficients(2, 640, 256)
    for copy in nz_image:
        copy.wait_recv()

    coefficients(1, 896, 384)
    text_rows(1, 1)
    pack_text(320, ROWS)
    near = [
        (
            send(left, text_send, PIECE * i, right_recv, PIECE * i, PIECE),
            send(right, text_send, HALF + PIECE * i, left_recv, HALF + PIECE * i, PIECE),
        )
        for i in range(2)
    ]
    coefficients(2, 896, 384)
    coefficients(0, 896, 384)
    image_rows(896, 384, 0, 3 * ROWS)
    for copy in y_last:
        copy.wait_recv()
    coefficients(3, 640, 640)
    image_rows(896, 384, 3 * ROWS, ROWS)
    image_send[pl.ds(640, ROWS), :] = packed(image_part[pl.ds(960, ROWS), :])
    nz_part = [send(after, image_send, 640 + PIECE * i, zn_recv, PIECE * i, PIECE) for i in range(4)]
    image_rows(640, 256, 0, BLOCK)
    text_rows(2, 0)
    z_part = [send(partner, image_send, 320 + PIECE * i, z_recv, PIECE * i, PIECE, False) for i in range(4)]

    def reduce_z(which, pieces):
        @pl.when(core == which)
        def _():
            for i in pieces:
                nz_part[i].wait_recv()
                rows = pl.ds(PIECE * i, PIECE)
                image_send[pl.ds(320 + PIECE * i, PIECE), :] = packed(
                    image_part[pl.ds(640 + PIECE * i, PIECE), :] + unpacked(zn_recv[rows, :])
                )
                z_part[i].start()

    reduce_z(1, range(4))
    text_rows(2, 1)
    pack_text(640, ROWS)
    mid = []
    for i in range(2):
        mid.append((
            send(left, text_send, 480 + PIECE * i, mid_recv, PIECE * i, PIECE),
            send(right, text_send, 320 + PIECE * i, mid_recv, HALF + PIECE * i, PIECE),
        ))
    last = []

    def reduce_y(i):
        pair = []
        for k, device, target, target_row in ((0, left, right_recv, HALF), (1, right, left_recv, 0)):
            mid[i][k].wait_recv()
            row = HALF * k + PIECE * i
            text_send[pl.ds(640 + row, PIECE), :] = packed(
                text_part[pl.ds(960 + row, PIECE), :] + unpacked(mid_recv[pl.ds(row, PIECE), :])
            )
            pair.append(send(device, text_send, 640 + row, target, target_row + PIECE * i, PIECE))
        last.append(pair)

    coefficients(3, 0, 640)
    image_rows(0, 640, 2 * ROWS, 2 * ROWS)
    image_send[pl.ds(0, ROWS), :] = packed(image_part[pl.ds(320, ROWS), :])
    n_part = send(after, image_send, 0, dn_recv, 0, ROWS)
    reduce_z(0, (0,))
    text_rows(3, 0)
    text_rows(3, 1)
    reduce_z(0, (1,))
    text_rows(0, 1)
    reduce_z(0, (2, 3))
    reduce_y(0)
    reduce_y(1)

    n_part.wait_recv()
    image_out[...] = image_part[pl.ds(0, ROWS), :] + unpacked(dn_recv[...])
    for i in range(2):
        for j in (2 * i, 2 * i + 1):
            z_part[j].wait_recv()
        rows = pl.ds(HALF * i, HALF)
        image_out[rows, :] += unpacked(z_recv[rows, :])
    for pair in near:
        for copy in pair:
            copy.wait_recv()
    text_out[pl.ds(0, HALF), :] = text_part[pl.ds(0, HALF), :] + unpacked(right_recv[pl.ds(0, HALF), :])
    text_out[pl.ds(HALF, HALF), :] = text_part[pl.ds(HALF, HALF), :] + unpacked(left_recv[pl.ds(HALF, HALF), :])
    for i in range(2):
        for k, source, row in ((0, right_recv, HALF), (1, left_recv, 0)):
            last[i][k].wait_recv()
            rows = pl.ds(row + PIECE * i, PIECE)
            text_out[rows, :] += unpacked(source[rows, :])
    for copy in copies:
        copy.wait_send()


def finish(image_ref, text_ref, image_out, text_out, sem):
    copies = [
        pltpu.make_async_copy(source, target, sem.at[k])
        for k, (source, target) in enumerate(((image_ref, image_out), (text_ref, text_out)))
    ]
    for copy in copies:
        copy.start()
    for copy in copies:
        copy.wait()


def per_device(image_embed, text_embed, logit_scale, logit_bias):
    half = lambda rows: pltpu.VMEM((rows, WIDTH), jnp.bfloat16)
    full = lambda rows: pltpu.VMEM((rows, WIDTH), jnp.float32)
    n_copies = 48
    out = pltpu.VMEM((ROWS, WIDTH), jnp.float32)
    sums = pl.pallas_call(
        kernel,
        out_shape=(out, out),
        in_specs=[pl.BlockSpec(memory_space=pltpu.SMEM)] * 2 + [pl.BlockSpec(memory_space=pltpu.HBM)] * 2,
        out_specs=(pl.BlockSpec(memory_space=pltpu.VMEM),) * 2,
        scratch_shapes=[
            full(ROWS), full(ROWS), half(BLOCK), half(BLOCK), pltpu.VMEM((BLOCK, BLOCK), jnp.bfloat16),
            full(BLOCK), full(BLOCK),
            half(3 * ROWS), half(3 * ROWS), half(ROWS), half(ROWS), half(ROWS), half(ROWS), half(ROWS), half(ROWS),
            pltpu.SemaphoreType.DMA((2,)),
            pltpu.SemaphoreType.DMA((n_copies,)), pltpu.SemaphoreType.DMA((n_copies,)),
        ],
        compiler_params=pltpu.CompilerParams(
            collective_id=0, has_side_effects=True, vmem_limit_bytes=60 * 2**20
        ),
        cost_estimate=pl.CostEstimate(
            flops=6 * BLOCK * BLOCK * WIDTH, bytes_accessed=16 * ROWS * WIDTH, transcendentals=BLOCK * BLOCK
        ),
    )(logit_scale.reshape(1), logit_bias.reshape(1), image_embed, text_embed)
    result = jax.ShapeDtypeStruct((ROWS, WIDTH), jnp.float32)
    return pl.pallas_call(
        finish,
        out_shape=(result, result),
        in_specs=[pl.BlockSpec(memory_space=pl.ANY)] * 2,
        out_specs=(pl.BlockSpec(memory_space=pl.ANY),) * 2,
        scratch_shapes=[pltpu.SemaphoreType.DMA((2,))],
        compiler_params=pltpu.CompilerParams(vmem_limit_bytes=2**20),
        cost_estimate=pl.CostEstimate(flops=0, bytes_accessed=16 * ROWS * WIDTH, transcendentals=0),
    )(*sums)


def solution(mesh):
    placed = (P(("node", "local"), None), P(("node", "local"), None), P(), P())
    return jax.shard_map(
        per_device,
        mesh=mesh,
        in_specs=placed,
        out_specs=(P(("node", "local"), None), P(("node", "local"), None)),
        check_vma=False,
    )
```

```python
import jax
import jax.numpy as jnp
from jax import lax
from jax.experimental import pallas as pl
from jax.experimental.pallas import tpu as pltpu
from jax.sharding import PartitionSpec as P

MESH = pl.DeviceIdType.MESH
ROWS, WIDTH = 320, 1152
HALF, PIECE = ROWS // 2, ROWS // 4
BLOCK = 4 * ROWS
NT = (((1,), (1,)), ((), ()))
TN = (((0,), (0,)), ((), ()))


def neighbours():
    node, local = lax.axis_index("node"), lax.axis_index("local")
    z_hi, x, core = node // 8, (node // 2) % 4, node % 2
    z_lo, y = local // 4, local % 4
    right = (node, z_lo * 4 + (y + 1) % 4)
    left = (node, z_lo * 4 + (y + 3) % 4)
    partner = (node, (1 - z_lo) * 4 + y)
    first = jnp.logical_and(core == 0, x == 0)
    last = jnp.logical_and(core == 1, x == 3)
    flipped = (1 - z_lo) * 4 + y
    before = ((node + 15) % 16, jnp.where(first, flipped, local))
    after = ((node + 1) % 16, jnp.where(last, flipped, local))
    return right, left, partner, before, after


def packed(value):
    square = value * value
    return (square * (value * jnp.abs(value))).astype(jnp.bfloat16)


def unpacked(power):
    power = power.astype(jnp.float32)
    root = lax.rsqrt(jnp.maximum(jnp.abs(power), 1e-37))
    return (power * root) * (root * lax.rsqrt(root))


def kernel(
    scale_ref, bias_ref, image_hbm, text_hbm, image_out, text_out,
    image_in, text_in, texts, images, coef, text_part, image_part,
    text_send, image_send, mid_recv, right_recv, left_recv, zn_recv, dn_recv, z_recv,
    load_sem, send_sem, recv_sem,
):
    right, left, partner, before, after = neighbours()
    core = lax.axis_index("node") % 2
    scale, bias = scale_ref[0], bias_ref[0]
    load_text = pltpu.make_async_copy(text_hbm, text_in, load_sem.at[0])
    load_image = pltpu.make_async_copy(image_hbm, image_in, load_sem.at[1])
    load_text.start()
    load_image.start()
    barrier = pltpu.get_barrier_semaphore()
    for device in (right, left, partner, before, after):
        pl.semaphore_signal(barrier, 1, device_id=device, device_id_type=MESH)

    copies = []

    def send(device, source, source_row, target, target_row, rows, start=True):
        k = len(copies)
        copy = pltpu.make_async_remote_copy(
            src_ref=source.at[pl.ds(source_row, rows)],
            dst_ref=target.at[pl.ds(target_row, rows)],
            send_sem=send_sem.at[k],
            recv_sem=recv_sem.at[k],
            device_id=device,
            device_id_type=MESH,
        )
        copies.append(copy)
        if start:
            copy.start()
        return copy

    def coefficients(group, lane, lanes):
        rows, place = pl.ds(group * ROWS, ROWS), pl.ds(lane, lanes)
        logits = scale * lax.dot_general(
            texts[rows, :], images[place, :], NT, preferred_element_type=jnp.float32
        ) + bias
        value = 1.0 / (1.0 + jnp.exp(-logits))
        if group == 0 and lane == 0:
            shape = (ROWS, lanes)
            match = lax.broadcasted_iota(jnp.int32, shape, 0) == lax.broadcasted_iota(jnp.int32, shape, 1)
            value = value - match.astype(jnp.float32)
        coef[rows, place] = (scale * value).astype(jnp.bfloat16)

    def text_rows(group, pair):
        rows, lanes = pl.ds(group * ROWS, ROWS), pl.ds(pair * 2 * ROWS, 2 * ROWS)
        part = jnp.dot(coef[rows, lanes], images[lanes, :], preferred_element_type=jnp.float32)
        if pair:
            part = text_part[rows, :] + part
        text_part[rows, :] = part

    def image_rows(lane, lanes, first, rows):
        place = pl.ds(lane, lanes)
        part = lax.dot_general(
            coef[pl.ds(first, rows), place], texts[pl.ds(first, rows), :], TN, preferred_element_type=jnp.float32
        )
        if first:
            part = image_part[place, :] + part
        image_part[place, :] = part

    def pack_text(row, rows):
        text_send[pl.ds(row - ROWS, rows), :] = packed(text_part[pl.ds(row, rows), :])

    load_text.wait()
    texts[pl.ds(0, ROWS), :] = text_in[...].astype(jnp.bfloat16)
    load_image.wait()
    images[pl.ds(0, ROWS), :] = image_in[...].astype(jnp.bfloat16)
    pl.semaphore_wait(barrier, 5)
    y_near = []
    for i in range(2):
        y_near.append((
            send(right, texts, PIECE * i, texts, 320 + PIECE * i, PIECE),
            send(left, texts, HALF + PIECE * i, texts, 480 + PIECE * i, PIECE),
        ))
    z_image = [send(partner, images, PIECE * i, images, 640 + PIECE * i, PIECE, False) for i in range(4)]
    nz_image = [send(before, images, 640 + PIECE * i, images, 960 + PIECE * i, PIECE, False) for i in range(4)]

    def start_z(which):
        @pl.when(core == which)
        def _():
            for copy in z_image:
                copy.start()

    def forward_z(which, pieces):
        @pl.when(core == which)
        def _():
            for i in pieces:
                z_image[i].wait_recv()
                nz_image[i].start()

    start_z(0)
    n_image = send(before, images, 0, images, 320, ROWS)
    y_far = []

    def forward_y(i):
        y_near[i][0].wait_recv()
        a = send(right, texts, 320 + PIECE * i, texts, 640 + PIECE * i, PIECE)
        y_near[i][1].wait_recv()
        b = send(left, texts, 480 + PIECE * i, texts, 800 + PIECE * i, PIECE)
        y_far.append((a, b))

    forward_y(0)
    start_z(1)
    forward_z(0, (0, 1))
    forward_y(1)
    y_last = (send(right, texts, HALF, texts, 960, HALF), send(left, texts, 0, texts, 1120, HALF))
    n_image.wait_recv()
    coefficients(0, 0, 640)
    coefficients(1, 0, 640)
    forward_z(0, (2,))
    forward_z(1, (0, 1))
    text_rows(1, 0)
    text_rows(0, 0)
    image_rows(0, 640, 0, 2 * ROWS)
    forward_z(0, (3,))
    forward_z(1, (2, 3))
    coefficients(1, 640, 256)
    coefficients(0, 640, 256)
    for i in range(2):
        for copy in y_far[i]:
            copy.wait_recv()
    coefficients(2, 0, 640)
    coefficients(2, 640, 256)
    text_rows(2, 0)
    for copy in nz_image:
        copy.wait_recv()

    coefficients(1, 896, 384)
    text_rows(1, 1)
    pack_text(320, ROWS)
    near = [
        (
            send(left, text_send, PIECE * i, right_recv, PIECE * i, PIECE),
            send(right, text_send, HALF + PIECE * i, left_recv, HALF + PIECE * i, PIECE),
        )
        for i in range(2)
    ]
    coefficients(2, 896, 384)
    coefficients(0, 896, 384)
    image_rows(896, 384, 0, 3 * ROWS)
    for copy in y_last:
        copy.wait_recv()
    coefficients(3, 640, 640)
    image_rows(896, 384, 3 * ROWS, ROWS)
    image_send[pl.ds(640, ROWS), :] = packed(image_part[pl.ds(960, ROWS), :])
    nz_part = [send(after, image_send, 640 + PIECE * i, zn_recv, PIECE * i, PIECE) for i in range(4)]
    image_rows(640, 256, 0, BLOCK)
    z_part = [send(partner, image_send, 320 + PIECE * i, z_recv, PIECE * i, PIECE, False) for i in range(4)]

    def reduce_z(which, pieces):
        @pl.when(core == which)
        def _():
            for i in pieces:
                nz_part[i].wait_recv()
                rows = pl.ds(PIECE * i, PIECE)
                image_send[pl.ds(320 + PIECE * i, PIECE), :] = packed(
                    image_part[pl.ds(640 + PIECE * i, PIECE), :] + unpacked(zn_recv[rows, :])
                )
                z_part[i].start()

    reduce_z(1, range(4))
    text_rows(2, 1)
    pack_text(640, ROWS)
    mid = []
    for i in range(2):
        mid.append((
            send(left, text_send, 480 + PIECE * i, mid_recv, PIECE * i, PIECE),
            send(right, text_send, 320 + PIECE * i, mid_recv, HALF + PIECE * i, PIECE),
        ))
    last = []

    def reduce_y(i):
        pair = []
        for k, device, target, target_row in ((0, left, right_recv, HALF), (1, right, left_recv, 0)):
            mid[i][k].wait_recv()
            row = HALF * k + PIECE * i
            text_send[pl.ds(640 + row, PIECE), :] = packed(
                text_part[pl.ds(960 + row, PIECE), :] + unpacked(mid_recv[pl.ds(row, PIECE), :])
            )
            pair.append(send(device, text_send, 640 + row, target, target_row + PIECE * i, PIECE))
        last.append(pair)

    coefficients(3, 0, 640)
    image_rows(0, 640, 2 * ROWS, 2 * ROWS)
    image_send[pl.ds(0, ROWS), :] = packed(image_part[pl.ds(320, ROWS), :])
    n_part = send(after, image_send, 0, dn_recv, 0, ROWS)
    reduce_z(0, (0,))
    text_rows(3, 0)
    text_rows(3, 1)
    reduce_z(0, (1,))
    text_rows(0, 1)
    reduce_z(0, (2, 3))
    reduce_y(0)
    image_out[...] = image_part[pl.ds(0, ROWS), :]
    for pair in near:
        for copy in pair:
            copy.wait_recv()
    text_out[pl.ds(0, HALF), :] = text_part[pl.ds(0, HALF), :] + unpacked(right_recv[pl.ds(0, HALF), :])
    text_out[pl.ds(HALF, HALF), :] = text_part[pl.ds(HALF, HALF), :] + unpacked(left_recv[pl.ds(HALF, HALF), :])
    reduce_y(1)

    def add_image(i):
        rows = pl.ds(HALF * i, HALF)
        for j in (2 * i, 2 * i + 1):
            z_part[j].wait_recv()
        image_out[rows, :] += unpacked(z_recv[rows, :])

    def add_text(i):
        for k, source, row in ((0, right_recv, HALF), (1, left_recv, 0)):
            last[i][k].wait_recv()
            rows = pl.ds(row + PIECE * i, PIECE)
            text_out[rows, :] += unpacked(source[rows, :])

    add_image(0)
    add_text(0)
    n_part.wait_recv()
    image_out[...] += unpacked(dn_recv[...])
    add_image(1)
    add_text(1)
    for copy in copies:
        copy.wait_send()


def finish(image_ref, text_ref, image_out, text_out, sem):
    copies = [
        pltpu.make_async_copy(source, target, sem.at[k])
        for k, (source, target) in enumerate(((image_ref, image_out), (text_ref, text_out)))
    ]
    for copy in copies:
        copy.start()
    for copy in copies:
        copy.wait()


def per_device(image_embed, text_embed, logit_scale, logit_bias):
    half = lambda rows: pltpu.VMEM((rows, WIDTH), jnp.bfloat16)
    full = lambda rows: pltpu.VMEM((rows, WIDTH), jnp.float32)
    n_copies = 48
    out = pltpu.VMEM((ROWS, WIDTH), jnp.float32)
    sums = pl.pallas_call(
        kernel,
        out_shape=(out, out),
        in_specs=[pl.BlockSpec(memory_space=pltpu.SMEM)] * 2 + [pl.BlockSpec(memory_space=pltpu.HBM)] * 2,
        out_specs=(pl.BlockSpec(memory_space=pltpu.VMEM),) * 2,
        scratch_shapes=[
            full(ROWS), full(ROWS), half(BLOCK), half(BLOCK), pltpu.VMEM((BLOCK, BLOCK), jnp.bfloat16),
            full(BLOCK), full(BLOCK),
            half(3 * ROWS), half(3 * ROWS), half(ROWS), half(ROWS), half(ROWS), half(ROWS), half(ROWS), half(ROWS),
            pltpu.SemaphoreType.DMA((2,)),
            pltpu.SemaphoreType.DMA((n_copies,)), pltpu.SemaphoreType.DMA((n_copies,)),
        ],
        compiler_params=pltpu.CompilerParams(
            collective_id=0, has_side_effects=True, vmem_limit_bytes=60 * 2**20
        ),
        cost_estimate=pl.CostEstimate(
            flops=6 * BLOCK * BLOCK * WIDTH, bytes_accessed=16 * ROWS * WIDTH, transcendentals=BLOCK * BLOCK
        ),
    )(logit_scale.reshape(1), logit_bias.reshape(1), image_embed, text_embed)
    result = jax.ShapeDtypeStruct((ROWS, WIDTH), jnp.float32)
    return pl.pallas_call(
        finish,
        out_shape=(result, result),
        in_specs=[pl.BlockSpec(memory_space=pl.ANY)] * 2,
        out_specs=(pl.BlockSpec(memory_space=pl.ANY),) * 2,
        scratch_shapes=[pltpu.SemaphoreType.DMA((2,))],
        compiler_params=pltpu.CompilerParams(vmem_limit_bytes=2**20),
        cost_estimate=pl.CostEstimate(flops=0, bytes_accessed=16 * ROWS * WIDTH, transcendentals=0),
    )(*sums)


def solution(mesh):
    placed = (P(("node", "local"), None), P(("node", "local"), None), P(), P())
    return jax.shard_map(
        per_device,
        mesh=mesh,
        in_specs=placed,
        out_specs=(P(("node", "local"), None), P(("node", "local"), None)),
        check_vma=False,
    )
```

```python
import jax
import jax.numpy as jnp
from jax import lax
from jax.experimental import pallas as pl
from jax.experimental.pallas import tpu as pltpu
from jax.sharding import PartitionSpec as P

MESH = pl.DeviceIdType.MESH
ROWS, WIDTH = 320, 1152
HALF, PIECE = ROWS // 2, ROWS // 4
BLOCK = 4 * ROWS
NT = (((1,), (1,)), ((), ()))
TN = (((0,), (0,)), ((), ()))


def neighbours():
    node, local = lax.axis_index("node"), lax.axis_index("local")
    z_hi, x, core = node // 8, (node // 2) % 4, node % 2
    z_lo, y = local // 4, local % 4
    right = (node, z_lo * 4 + (y + 1) % 4)
    left = (node, z_lo * 4 + (y + 3) % 4)
    partner = (node, (1 - z_lo) * 4 + y)
    first = jnp.logical_and(core == 0, x == 0)
    last = jnp.logical_and(core == 1, x == 3)
    flipped = (1 - z_lo) * 4 + y
    before = ((node + 15) % 16, jnp.where(first, flipped, local))
    after = ((node + 1) % 16, jnp.where(last, flipped, local))
    return right, left, partner, before, after


def packed(value):
    square = value * value
    return (square * (value * jnp.abs(value))).astype(jnp.bfloat16)


def unpacked(power):
    power = power.astype(jnp.float32)
    root = lax.rsqrt(jnp.maximum(jnp.abs(power), 1e-37))
    return (power * root) * (root * lax.rsqrt(root))


def kernel(
    scale_ref, bias_ref, image_hbm, text_hbm, image_out, text_out,
    image_in, text_in, texts, images, coef, text_part, image_part,
    text_send, image_send, mid_recv, right_recv, left_recv, zn_recv, dn_recv, z_recv,
    load_sem, send_sem, recv_sem,
):
    right, left, partner, before, after = neighbours()
    core = lax.axis_index("node") % 2
    scale, bias = scale_ref[0], bias_ref[0]
    load_text = pltpu.make_async_copy(text_hbm, text_in, load_sem.at[0])
    load_image = pltpu.make_async_copy(image_hbm, image_in, load_sem.at[1])
    load_text.start()
    load_image.start()
    barrier = pltpu.get_barrier_semaphore()
    for device in (right, left, partner, before, after):
        pl.semaphore_signal(barrier, 1, device_id=device, device_id_type=MESH)

    copies = []

    def send(device, source, source_row, target, target_row, rows, start=True):
        k = len(copies)
        copy = pltpu.make_async_remote_copy(
            src_ref=source.at[pl.ds(source_row, rows)],
            dst_ref=target.at[pl.ds(target_row, rows)],
            send_sem=send_sem.at[k],
            recv_sem=recv_sem.at[k],
            device_id=device,
            device_id_type=MESH,
        )
        copies.append(copy)
        if start:
            copy.start()
        return copy

    def coefficients(group, lane, lanes):
        rows, place = pl.ds(group * ROWS, ROWS), pl.ds(lane, lanes)
        logits = scale * lax.dot_general(
            texts[rows, :], images[place, :], NT, preferred_element_type=jnp.float32
        ) + bias
        value = 1.0 / (1.0 + jnp.exp(-logits))
        if group == 0 and lane == 0:
            shape = (ROWS, lanes)
            match = lax.broadcasted_iota(jnp.int32, shape, 0) == lax.broadcasted_iota(jnp.int32, shape, 1)
            value = value - match.astype(jnp.float32)
        coef[rows, place] = (scale * value).astype(jnp.bfloat16)

    def text_rows(group, pair):
        rows, lanes = pl.ds(group * ROWS, ROWS), pl.ds(pair * 2 * ROWS, 2 * ROWS)
        part = jnp.dot(coef[rows, lanes], images[lanes, :], preferred_element_type=jnp.float32)
        if pair:
            part = text_part[rows, :] + part
        text_part[rows, :] = part

    def image_rows(lane, lanes, first, rows):
        place = pl.ds(lane, lanes)
        part = lax.dot_general(
            coef[pl.ds(first, rows), place], texts[pl.ds(first, rows), :], TN, preferred_element_type=jnp.float32
        )
        if first:
            part = image_part[place, :] + part
        image_part[place, :] = part

    def pack_text(row, rows):
        text_send[pl.ds(row - ROWS, rows), :] = packed(text_part[pl.ds(row, rows), :])

    load_text.wait()
    texts[pl.ds(0, ROWS), :] = text_in[...].astype(jnp.bfloat16)
    load_image.wait()
    images[pl.ds(0, ROWS), :] = image_in[...].astype(jnp.bfloat16)
    pl.semaphore_wait(barrier, 5)
    y_near = []
    for i in range(2):
        y_near.append((
            send(right, texts, PIECE * i, texts, 320 + PIECE * i, PIECE),
            send(left, texts, HALF + PIECE * i, texts, 480 + PIECE * i, PIECE),
        ))
    z_image = [send(partner, images, PIECE * i, images, 640 + PIECE * i, PIECE, False) for i in range(4)]
    nz_image = [send(before, images, 640 + PIECE * i, images, 960 + PIECE * i, PIECE, False) for i in range(4)]

    def start_z(which):
        @pl.when(core == which)
        def _():
            for copy in z_image:
                copy.start()

    def forward_z(which, pieces):
        @pl.when(core == which)
        def _():
            for i in pieces:
                z_image[i].wait_recv()
                nz_image[i].start()

    start_z(0)
    n_image = send(before, images, 0, images, 320, ROWS)
    y_far = []

    def forward_y(i):
        y_near[i][0].wait_recv()
        a = send(right, texts, 320 + PIECE * i, texts, 640 + PIECE * i, PIECE)
        y_near[i][1].wait_recv()
        b = send(left, texts, 480 + PIECE * i, texts, 800 + PIECE * i, PIECE)
        y_far.append((a, b))

    start_z(1)
    forward_y(0)
    forward_z(0, (0, 1))
    forward_y(1)
    y_last = (send(right, texts, HALF, texts, 960, HALF), send(left, texts, 0, texts, 1120, HALF))
    n_image.wait_recv()
    coefficients(0, 0, 640)
    coefficients(1, 0, 640)
    forward_z(0, (2,))
    forward_z(1, (0, 1))
    text_rows(1, 0)
    text_rows(0, 0)
    image_rows(0, 640, 0, 2 * ROWS)
    forward_z(0, (3,))
    forward_z(1, (2, 3))
    coefficients(1, 640, 256)
    coefficients(0, 640, 256)
    for i in range(2):
        for copy in y_far[i]:
            copy.wait_recv()
    coefficients(2, 0, 640)
    coefficients(2, 640, 256)
    text_rows(2, 0)
    for copy in nz_image:
        copy.wait_recv()

    coefficients(1, 896, 384)
    text_rows(1, 1)
    pack_text(320, ROWS)
    near = [
        (
            send(left, text_send, PIECE * i, right_recv, PIECE * i, PIECE),
            send(right, text_send, HALF + PIECE * i, left_recv, HALF + PIECE * i, PIECE),
        )
        for i in range(2)
    ]
    coefficients(2, 896, 384)
    coefficients(0, 896, 384)
    image_rows(896, 384, 0, 3 * ROWS)
    for copy in y_last:
        copy.wait_recv()
    coefficients(3, 640, 640)
    image_rows(896, 384, 3 * ROWS, ROWS)
    image_send[pl.ds(640, ROWS), :] = packed(image_part[pl.ds(960, ROWS), :])
    nz_part = [send(after, image_send, 640 + PIECE * i, zn_recv, PIECE * i, PIECE) for i in range(4)]
    image_rows(640, 256, 0, BLOCK)
    z_part = [send(partner, image_send, 320 + PIECE * i, z_recv, PIECE * i, PIECE, False) for i in range(4)]

    def reduce_z(which, pieces):
        @pl.when(core == which)
        def _():
            for i in pieces:
                nz_part[i].wait_recv()
                rows = pl.ds(PIECE * i, PIECE)
                image_send[pl.ds(320 + PIECE * i, PIECE), :] = packed(
                    image_part[pl.ds(640 + PIECE * i, PIECE), :] + unpacked(zn_recv[rows, :])
                )
                z_part[i].start()

    reduce_z(1, range(4))
    text_rows(2, 1)
    pack_text(640, ROWS)
    mid = []
    for i in range(2):
        mid.append((
            send(left, text_send, 480 + PIECE * i, mid_recv, PIECE * i, PIECE),
            send(right, text_send, 320 + PIECE * i, mid_recv, HALF + PIECE * i, PIECE),
        ))
    last = []

    def reduce_y(i):
        pair = []
        for k, device, target, target_row in ((0, left, right_recv, HALF), (1, right, left_recv, 0)):
            mid[i][k].wait_recv()
            row = HALF * k + PIECE * i
            text_send[pl.ds(640 + row, PIECE), :] = packed(
                text_part[pl.ds(960 + row, PIECE), :] + unpacked(mid_recv[pl.ds(row, PIECE), :])
            )
            pair.append(send(device, text_send, 640 + row, target, target_row + PIECE * i, PIECE))
        last.append(pair)

    coefficients(3, 0, 640)
    image_rows(0, 640, 2 * ROWS, 2 * ROWS)
    image_send[pl.ds(0, ROWS), :] = packed(image_part[pl.ds(320, ROWS), :])
    n_part = send(after, image_send, 0, dn_recv, 0, ROWS)
    reduce_z(0, (0,))
    text_rows(3, 0)
    text_rows(3, 1)
    reduce_z(0, (1,))
    text_rows(0, 1)
    reduce_z(0, (2, 3))
    reduce_y(0)
    image_out[...] = image_part[pl.ds(0, ROWS), :]
    for pair in near:
        for copy in pair:
            copy.wait_recv()
    text_out[pl.ds(0, HALF), :] = text_part[pl.ds(0, HALF), :] + unpacked(right_recv[pl.ds(0, HALF), :])
    text_out[pl.ds(HALF, HALF), :] = text_part[pl.ds(HALF, HALF), :] + unpacked(left_recv[pl.ds(HALF, HALF), :])
    reduce_y(1)

    def add_image(i):
        rows = pl.ds(HALF * i, HALF)
        for j in (2 * i, 2 * i + 1):
            z_part[j].wait_recv()
        image_out[rows, :] += unpacked(z_recv[rows, :])

    def add_text(i):
        for k, source, row in ((0, right_recv, HALF), (1, left_recv, 0)):
            last[i][k].wait_recv()
            rows = pl.ds(row + PIECE * i, PIECE)
            text_out[rows, :] += unpacked(source[rows, :])

    add_image(0)
    add_text(0)
    n_part.wait_recv()
    image_out[...] += unpacked(dn_recv[...])
    add_image(1)
    add_text(1)
    for copy in copies:
        copy.wait_send()


def finish(image_ref, text_ref, image_out, text_out, sem):
    copies = [
        pltpu.make_async_copy(source, target, sem.at[k])
        for k, (source, target) in enumerate(((image_ref, image_out), (text_ref, text_out)))
    ]
    for copy in copies:
        copy.start()
    for copy in copies:
        copy.wait()


def per_device(image_embed, text_embed, logit_scale, logit_bias):
    half = lambda rows: pltpu.VMEM((rows, WIDTH), jnp.bfloat16)
    full = lambda rows: pltpu.VMEM((rows, WIDTH), jnp.float32)
    n_copies = 48
    out = pltpu.VMEM((ROWS, WIDTH), jnp.float32)
    sums = pl.pallas_call(
        kernel,
        out_shape=(out, out),
        in_specs=[pl.BlockSpec(memory_space=pltpu.SMEM)] * 2 + [pl.BlockSpec(memory_space=pltpu.HBM)] * 2,
        out_specs=(pl.BlockSpec(memory_space=pltpu.VMEM),) * 2,
        scratch_shapes=[
            full(ROWS), full(ROWS), half(BLOCK), half(BLOCK), pltpu.VMEM((BLOCK, BLOCK), jnp.bfloat16),
            full(BLOCK), full(BLOCK),
            half(3 * ROWS), half(3 * ROWS), half(ROWS), half(ROWS), half(ROWS), half(ROWS), half(ROWS), half(ROWS),
            pltpu.SemaphoreType.DMA((2,)),
            pltpu.SemaphoreType.DMA((n_copies,)), pltpu.SemaphoreType.DMA((n_copies,)),
        ],
        compiler_params=pltpu.CompilerParams(
            collective_id=0, has_side_effects=True, vmem_limit_bytes=60 * 2**20
        ),
        cost_estimate=pl.CostEstimate(
            flops=6 * BLOCK * BLOCK * WIDTH, bytes_accessed=16 * ROWS * WIDTH, transcendentals=BLOCK * BLOCK
        ),
    )(logit_scale.reshape(1), logit_bias.reshape(1), image_embed, text_embed)
    result = jax.ShapeDtypeStruct((ROWS, WIDTH), jnp.float32)
    return pl.pallas_call(
        finish,
        out_shape=(result, result),
        in_specs=[pl.BlockSpec(memory_space=pl.ANY)] * 2,
        out_specs=(pl.BlockSpec(memory_space=pl.ANY),) * 2,
        scratch_shapes=[pltpu.SemaphoreType.DMA((2,))],
        compiler_params=pltpu.CompilerParams(vmem_limit_bytes=2**20),
        cost_estimate=pl.CostEstimate(flops=0, bytes_accessed=16 * ROWS * WIDTH, transcendentals=0),
    )(*sums)


def solution(mesh):
    placed = (P(("node", "local"), None), P(("node", "local"), None), P(), P())
    return jax.shard_map(
        per_device,
        mesh=mesh,
        in_specs=placed,
        out_specs=(P(("node", "local"), None), P(("node", "local"), None)),
        check_vma=False,
    )
```
